256 devices in a mesh: section: 8 (over z_lo, core), tensor: 32 (over z_hi, y, x).
Axes of the slice: x: 4, y: 4, z: 8 (z_hi: 2, z_lo: 4; z = z_hi * 4 + z_lo), core: 2. Of those that a mesh axis runs over, the one named last changes fastest.
Arguments:
- held: bfloat16 [8, 4, 256, 2048], P('section', None, 'tensor'), may hold values from -6 to 6
- head: bfloat16 [4, 256, 2048], P(None, 'tensor'), may hold values from -6 to 6
- gains: float32 [8, 2, 2048], P('section'), may hold values from 0.1 to 1.9
- w_in: bfloat16 [8, 2, 2048, 8192], P('section', None, None, 'tensor'), may hold values from -0.125 to 0.125
- w_out: bfloat16 [8, 2, 8192, 2048], P('section', None, 'tensor'), may hold values from -0.0625 to 0.0625
- masks: int32 [8, 2, 2, 256, 8192], P('section', None, None, None, 'tensor'), may hold values 0 or 1
Outputs:
- rebuilt: bfloat16 [8, 2, 4, 256, 2048], P('section', None, None, 'tensor')
- grad_w_in: bfloat16 [8, 2, 2048, 8192], P('section', None, None, 'tensor')
- grad_w_out: bfloat16 [8, 2, 8192, 2048], P('section', None, 'tensor')
- grad_gains: float32 [8, 2, 2048], P('section')
The draws below stay inside these ranges and needn't reach their ends.
Inputs may be any that keep to these rules, and one draw needn't show every extreme that they name: `masks`: 1 keeps a hidden unit, 0 drops it.
All inputs are finite; a program needn't handle non-finite values. No bound on the sum of `masks` on one device may be relied on, other than what follows from the above.
Results may differ from the reference program's by a relative error of at most 0.04.
Values may be sent and summed in bfloat16 or wider, within the bound.
A program may use at most 128 MiB of HBM per device.

```python
import math
import jax
import jax.numpy as jnp
from jax import lax

D = 2048
FF = 8192
TOK = 256
TICKS = 2
LAYERS = 2
SECTIONS = 8
N_SECTION = 8
N_TENSOR = 32


def place_ends(values, key, least, largest):
    place = [jax.random.randint(jax.random.fold_in(key, axis), (), 0, length) for axis, length in enumerate(values.shape)]
    longest = values.shape.index(max(values.shape))
    next_to = place[:longest] + [(place[longest] + 1) % values.shape[longest]] + place[longest + 1:]
    return values.at[tuple(place)].set(least).at[tuple(next_to)].set(largest)


def shard_levels(rng, dims, cuts, smallest, top_value):
    level = 1.0
    for position, shards_of in cuts:
        steps = jax.random.uniform(jax.random.fold_in(jax.random.fold_in(rng, 6), position), (shards_of,), jnp.float32, smallest / len(cuts), top_value / len(cuts))
        level = level * jnp.repeat(jnp.exp(steps), dims[position] // shards_of).reshape((-1,) + (1,) * (len(dims) - 1 - position))
    return level


def noise(rng, extent, width, reach, cuts=(), held_as=jnp.bfloat16):
    drawn = width * jax.random.normal(rng, extent, jnp.float32)
    if cuts:
        drawn = drawn * shard_levels(rng, extent, cuts, -0.22, 0.18)
    return jnp.clip(drawn, -reach, reach).astype(held_as)


def setup_inputs(seed: int = 0) -> dict:
    streams_of = jax.random.split(jax.random.key(seed), 7)
    return {
        "held": noise(streams_of[0], (SECTIONS, 4, TOK, D), 1.0, 6.0, ((0, 8), (2, 32))),
        "head": noise(streams_of[1], (4, TOK, D), 1.0, 6.0, ((1, 32),)),
        "gains": jnp.clip(1.0 + 0.18 * jax.random.normal(streams_of[2], (SECTIONS, LAYERS, D), jnp.float32), 0.1, 1.9),
        "w_in": noise(streams_of[3], (SECTIONS, LAYERS, D, FF), D ** -0.5, 0.125, ((0, 8), (3, 32))),
        "w_out": noise(streams_of[4], (SECTIONS, LAYERS, FF, D), FF ** -0.5, 0.0625, ((0, 8), (2, 32))),
        "masks": place_ends((jax.random.randint(streams_of[5], (SECTIONS, TICKS, LAYERS, TOK, FF), 0, 10) < 9).astype(jnp.int32), jax.random.fold_in(streams_of[5], 1), 0, 1),
    }


KEEP = 0.9
EPS = 1e-05
CUBIC = 0.044715
ROOT = math.sqrt(2.0 / math.pi)

def gelu_value(hidden):
    inner = ROOT * (hidden + CUBIC * hidden * hidden * hidden)
    return 0.5 * hidden * (1.0 + jnp.tanh(inner))

def gelu_slope(hidden):
    inner = ROOT * (hidden + CUBIC * hidden * hidden * hidden)
    tangent = jnp.tanh(inner)
    return 0.5 * (1.0 + tangent) + 0.5 * hidden * (1.0 - tangent * tangent) * ROOT * (1.0 + 3.0 * CUBIC * hidden * hidden)

def blocked_sum(left, right):

    def step(total, pair):
        part = jnp.dot(pair[0], pair[1], preferred_element_type=jnp.float32)
        part = lax.optimization_barrier(part.astype(jnp.bfloat16))
        return (total + part.astype(jnp.float32), None)
    start = jnp.zeros((left.shape[1], right.shape[2]), jnp.float32)
    total, _ = lax.scan(step, start, (left, right))
    return total

def branch_forward(inputs, gain, w_first, w_second, mask):
    wide = inputs.astype(jnp.float32)
    scale = lax.rsqrt(lax.optimization_barrier(jnp.mean(wide * wide, axis=-1, keepdims=True)) + EPS)
    unit = wide * scale
    normed = (unit * gain).astype(jnp.bfloat16)
    hidden = jnp.dot(normed, w_first, preferred_element_type=jnp.float32)
    keep_mask = mask.astype(jnp.float32) / KEEP
    active = (gelu_value(hidden) * keep_mask).astype(jnp.bfloat16)
    rows = inputs.shape[0]
    left = active.reshape(rows, N_TENSOR, -1).transpose(1, 0, 2)
    right = w_second.reshape(N_TENSOR, -1, w_second.shape[1])
    branch = blocked_sum(left, right)
    return (branch, (scale, unit, normed, hidden, keep_mask, active))

def branch_backward(grad, gain, w_first, w_second, saved):
    scale, unit, normed, hidden, keep_mask, active = saved
    back_active = jnp.dot(grad, w_second.T, preferred_element_type=jnp.float32)
    back_hidden = (back_active * keep_mask * gelu_slope(hidden)).astype(jnp.bfloat16)
    term_out = jnp.dot(active.T, grad, preferred_element_type=jnp.float32)
    term_in = jnp.dot(normed.T, back_hidden, preferred_element_type=jnp.float32)
    rows = grad.shape[0]
    left = back_hidden.reshape(rows, N_TENSOR, -1).transpose(1, 0, 2)
    right = w_first.reshape(w_first.shape[0], N_TENSOR, -1).transpose(1, 2, 0)
    back_normed = blocked_sum(left, right)
    term_gain = lax.optimization_barrier(jnp.sum(back_normed * unit, axis=0))
    back_unit = back_normed * gain
    back_input = scale * (back_unit - unit * lax.optimization_barrier(jnp.mean(back_unit * unit, axis=-1, keepdims=True)))
    return (back_input, term_in, term_out, term_gain)

def section_backward(inputs, gain, w_first, w_second, mask):
    out_one, out_two, grad_one, grad_two = (inputs[0], inputs[1], inputs[2], inputs[3])
    branch_two, saved_two = branch_forward(out_one, gain[1], w_first[1], w_second[1], mask[1])
    in_two = (out_two.astype(jnp.float32) - branch_two).astype(jnp.bfloat16)
    branch_one, saved_one = branch_forward(in_two, gain[0], w_first[0], w_second[0], mask[0])
    in_one = (out_one.astype(jnp.float32) - branch_one).astype(jnp.bfloat16)
    back_two, in_b, out_b, gain_b = branch_backward(grad_two, gain[1], w_first[1], w_second[1], saved_two)
    grad_in_one = (grad_one.astype(jnp.float32) + back_two).astype(jnp.bfloat16)
    back_one, in_a, out_a, gain_a = branch_backward(grad_in_one, gain[0], w_first[0], w_second[0], saved_one)
    grad_in_two = (grad_two.astype(jnp.float32) + back_one).astype(jnp.bfloat16)
    rebuilt = jnp.stack([in_one, in_two, grad_in_one, grad_in_two])
    return (rebuilt, jnp.stack([in_a, in_b]), jnp.stack([out_a, out_b]), jnp.stack([gain_a, gain_b]))

def reference(held, head, gains, w_in, w_out, masks):
    first = []
    sums = []
    for section in range(N_SECTION):
        result = section_backward(held[section], gains[section], w_in[section], w_out[section], masks[section, 0])
        first.append(result[0])
        sums.append(result[1:])
    rebuilt = []
    grads_in = []
    grads_out = []
    grads_gain = []
    for section in range(N_SECTION):
        source = head if section == N_SECTION - 1 else first[section + 1]
        result = section_backward(source, gains[section], w_in[section], w_out[section], masks[section, 1])
        rebuilt.append(jnp.stack([first[section], result[0]]))
        grads_in.append((sums[section][0] + result[1]).astype(jnp.bfloat16))
        grads_out.append((sums[section][1] + result[2]).astype(jnp.bfloat16))
        grads_gain.append(sums[section][2] + result[3])
    return (jnp.stack(rebuilt), jnp.stack(grads_in), jnp.stack(grads_out), jnp.stack(grads_gain))
```

```python
import math

import jax
import jax.numpy as jnp
from jax import lax
from jax.experimental import pallas as pl
from jax.experimental.pallas import tpu as pltpu
from jax.sharding import PartitionSpec as P

KEEP = 0.9
EPS = 1e-05
CUBIC = 0.044715
ROOT = math.sqrt(2.0 / math.pi)
MESH = pl.DeviceIdType.MESH
F32 = jnp.float32
BF16 = jnp.bfloat16
FWD, BWD = 0, 1
HALF = 1024
OFFSETS = (2, 1, 3)


def dot_nn(a, b):
    return lax.dot_general(a, b, (((1,), (0,)), ((), ())), preferred_element_type=F32)


def dot_nt(a, b):
    return lax.dot_general(a, b, (((1,), (1,)), ((), ())), preferred_element_type=F32)


def dot_tn(a, b):
    return lax.dot_general(a, b, (((0,), (0,)), ((), ())), preferred_element_type=F32)


def kernel(
    held, head, gains, w_in_hbm, w_out_hbm, masks_hbm,
    rebuilt, grad_in_hbm, grad_out_hbm, grad_gains,
    w_in, w_out, masks, gath, part, r1, s1, r2, zs, zr, rows, act_t, back_h, slope_k,
    gw_in, gw_out, hs, hr, gsum, grx, gry,
    ag1_s, ag1_r, agx_s, agx_r, ag2_s, ag2_r, rs1_s, rs1_r, rs2_s, rs2_r, z_s, z_r,
    tick_s, tick_r, hs_s, hs_r, gx_s, gx_r, load_s, out_s,
):
    sec = lax.axis_index("section")
    me = lax.axis_index("tensor")
    last = lax.axis_size("section") - 1
    x = lax.rem(me, 4)
    y = lax.rem(me // 4, 4)
    z = me // 16

    def x_peer(d):
        return {"tensor": z * 16 + y * 4 + lax.rem(x + d, 4)}

    def y_peer(d):
        return {"tensor": z * 16 + lax.rem(y + d, 4) * 4 + x}

    z_peer = {"tensor": lax.rem(me + 16, 32)}

    def send(src, dst, s_sem, r_sem, device):
        pltpu.make_async_remote_copy(
            src_ref=src, dst_ref=dst, send_sem=s_sem, recv_sem=r_sem,
            device_id=device, device_id_type=MESH,
        ).start()

    def wait(ref, sem):
        pltpu.make_async_copy(ref, ref, sem).wait()

    loads = [
        pltpu.make_async_copy(w_in_hbm, w_in, load_s.at[0]),
        pltpu.make_async_copy(w_out_hbm, w_out, load_s.at[1]),
    ]
    for dy in range(4):
        for dx in range(4):
            block = lax.rem(y + dy, 4) * 4 + lax.rem(x + dx, 4)
            loads.append(
                pltpu.make_async_copy(
                    masks_hbm.at[:, :, :, block], masks.at[:, :, dy * 4 + dx], load_s.at[2 + dy * 4 + dx]
                )
            )
    for copy in loads:
        copy.start()

    barrier = pltpu.get_barrier_semaphore()
    for d in (1, 2, 3):
        pl.semaphore_signal(barrier, inc=1, device_id=x_peer(d), device_id_type=MESH)
        pl.semaphore_signal(barrier, inc=1, device_id=y_peer(d), device_id_type=MESH)
    pl.semaphore_signal(barrier, inc=1, device_id=z_peer, device_id_type=MESH)

    above = {"section": lax.rem(sec + 1, last + 1)}
    pl.semaphore_signal(barrier, inc=1, device_id=above, device_id_type=MESH)

    def pack(source, slot):
        for j in range(4):
            v = source[j].astype(F32)
            hs[slot, j] = jnp.concatenate([v[:, :HALF], v[:, HALF:]], axis=0).astype(BF16)

    pack(held, 0)

    pl.semaphore_wait(barrier, 8)

    places = ((0, FWD, 1), (3, BWD, 1), (1, FWD, 0), (2, BWD, 0))
    for j, _, _ in places:
        send(hs.at[0, j], hr.at[0, j], hs_s.at[j], hs_r.at[j], z_peer)

    @pl.when(sec == last)
    def _():
        pack(head, 1)
        for j, _, _ in places:
            send(hs.at[1, j], hr.at[1, j], hs_s.at[4 + j], hs_r.at[4 + j], z_peer)

    def unpack(slot, j, tick, chain, place):
        wait(hr.at[slot, j], hs_r.at[4 * slot + j])
        mine = hs[slot, j].astype(F32)
        theirs = hr[slot, j].astype(F32)
        for h in range(2):
            a = mine[8 * h : 8 * h + 8]
            b = theirs[8 * h : 8 * h + 8]
            both = jnp.concatenate([jnp.where(z == 0, a, b), jnp.where(z == 0, b, a)], axis=0)
            rows[tick, chain, place, h] = both.astype(BF16)

    def gain_row(layer):
        pair = gains[0]
        return jnp.where(layer == 1, pair[1:2], pair[0:1])

    def norm_of(tick, place):
        v0 = rows[tick, FWD, place, 0].astype(F32)
        v1 = rows[tick, FWD, place, 1].astype(F32)
        total = jnp.sum(v0 * v0, axis=-1, keepdims=True) + jnp.sum(v1 * v1, axis=-1, keepdims=True)
        scale = lax.rsqrt(total * (1.0 / (2 * HALF)) + EPS)
        return scale, (v0 * scale, v1 * scale)

    def gather_start(chain, s):
        for d in OFFSETS:
            send(gath.at[s, chain, 0, 0, 0], gath.at[s, chain, 0, 0, 4 - d], ag1_s.at[chain, 0], ag1_r.at[chain, 0], x_peer(d))
            send(gath.at[s, chain, 1, 0, 0], gath.at[s, chain, 1, 4 - d, 0], ag1_s.at[chain, 1], ag1_r.at[chain, 1], y_peer(d))
        for d in OFFSETS:
            send(gath.at[s, chain, 0, 0, 0], gath.at[s, chain, 0, 4 - d, 0], agx_s.at[chain, 0], agx_r.at[chain, 0], y_peer(d))
            send(gath.at[s, chain, 1, 0, 0], gath.at[s, chain, 1, 0, 4 - d], agx_s.at[chain, 1], agx_r.at[chain, 1], x_peer(d))

    def gather_mid(chain, s):
        wait(gath.at[s, chain, 0, 0, pl.ds(1, 3)], ag1_r.at[chain, 0])
        for d in OFFSETS:
            send(
                gath.at[s, chain, 0, 0, pl.ds(1, 3)], gath.at[s, chain, 0, 4 - d, pl.ds(1, 3)],
                ag2_s.at[chain, 0], ag2_r.at[chain, 0], y_peer(d),
            )
        wait(gath.at[s, chain, 1, pl.ds(1, 3), 0], ag1_r.at[chain, 1])
        for d in OFFSETS:
            send(
                gath.at[s, chain, 1, pl.ds(1, 3), 0], gath.at[s, chain, 1, pl.ds(1, 3), 4 - d],
                ag2_s.at[chain, 1], ag2_r.at[chain, 1], x_peer(d),
            )

    def gather_wait(chain, s, h):
        wait(gath.at[s, chain, h, 0, pl.ds(1, 3)], agx_r.at[chain, h])
        wait(gath.at[s, chain, h, pl.ds(1, 3), pl.ds(1, 3)], ag2_r.at[chain, h])

    def gather_sent(chain, s):
        for h in range(2):
            wait(gath.at[s, chain, h, 0, pl.ds(1, 3)], ag1_s.at[chain, h])
            wait(gath.at[s, chain, h, 0, pl.ds(1, 3)], agx_s.at[chain, h])
            wait(gath.at[s, chain, h, pl.ds(1, 3), pl.ds(1, 3)], ag2_s.at[chain, h])

    def gathered(chain, s, h):
        return gath[s, chain, h].reshape(256, HALF)

    def put_part(chain, h, value):
        part[chain, h] = value.astype(BF16).reshape(4, 4, 16, HALF)
        for d in OFFSETS:
            if h == 0:
                send(part.at[chain, 0, :, d], r1.at[chain, 0, d - 1], rs1_s.at[chain, 0], rs1_r.at[chain, 0], x_peer(d))
            else:
                send(part.at[chain, 1, d], r1.at[chain, 1, d - 1], rs1_s.at[chain, 1], rs1_r.at[chain, 1], y_peer(d))

    def sum_mid(chain):
        for h in range(2):
            wait(r1.at[chain, h], rs1_r.at[chain, h])
            for d in OFFSETS + (0,):
                own = part[chain, 0, d, 0] if h == 0 else part[chain, 1, 0, d]
                total = own.astype(F32)
                for j in range(3):
                    total = total + r1[chain, h, j, d].astype(F32)
                s1[chain, h, d] = total.astype(BF16)
                if d:
                    send(
                        s1.at[chain, h, d], r2.at[chain, h, d - 1], rs2_s.at[chain, h], rs2_r.at[chain, h],
                        y_peer(d) if h == 0 else x_peer(d),
                    )

    def sum_end(chain, k):
        for h in range(2):
            wait(r2.at[chain, h], rs2_r.at[chain, h])
            total = s1[chain, h, 0].astype(F32)
            for j in range(3):
                total = total + r2[chain, h, j].astype(F32)
            zs[chain, h] = total.astype(BF16)
        send(zs.at[chain], zr.at[k, chain], z_s.at[chain], z_r.at[k, chain], z_peer)

    def sum_sent(chain):
        for h in range(2):
            wait(r1.at[chain, h], rs1_s.at[chain, h])
            wait(r2.at[chain, h], rs2_s.at[chain, h])
        wait(zs.at[chain], z_s.at[chain])

    def whole_sum(chain, k):
        wait(zr.at[k, chain], z_r.at[k, chain])
        return [zs[chain, h].astype(F32) + zr[k, chain, h].astype(F32) for h in range(2)]

    def begin(chain, s):
        tick, k = s // 2, lax.rem(s, 2)
        if chain == FWD:
            gain = gain_row(1 - k)
            _, unit = norm_of(tick, k + 1)
            for h in range(2):
                gath[s, FWD, h, 0, 0] = (unit[h] * gain[:, h * HALF : (h + 1) * HALF]).astype(BF16)
        else:
            for h in range(2):
                gath[s, BWD, h, 0, 0] = rows[tick, BWD, k + 1, h]
        gather_start(chain, s)

    def hand_on(chain, k):
        @pl.when(sec > 0)
        def _():
            send(
                rows.at[0, chain, k + 2], rows.at[1, chain, k], tick_s.at[chain, k], tick_r.at[chain, k],
                {"section": sec - 1},
            )

    def take_over(chain):
        @pl.when(sec < last)
        def _():
            for k in range(2):
                wait(rows.at[1, chain, k], tick_r.at[chain, k])

    gsum[...] = jnp.zeros_like(gsum)

    for j, chain, place in places[:2]:
        unpack(0, j, 0, chain, place)
        begin(chain, 0)
    for j, chain, place in places[2:]:
        unpack(0, j, 0, chain, place)

    @pl.when(sec == last)
    def _():
        for j, chain, place in places:
            unpack(1, j, 1, chain, place)

    for copy in loads:
        copy.wait()

    def step(s, carry):
        tick, k = s // 2, lax.rem(s, 2)
        layer = 1 - k

        gather_mid(FWD, s)
        gather_mid(BWD, s)

        gather_wait(FWD, s, 0)
        hidden = dot_nn(gathered(FWD, s, 0), w_in[layer, pl.ds(0, HALF)])
        gather_wait(FWD, s, 1)
        hidden = hidden + dot_nn(gathered(FWD, s, 1), w_in[layer, pl.ds(HALF, HALF)])
        keep = masks[tick, layer].reshape(256, 256).astype(F32) * (1.0 / KEEP)
        square = hidden * hidden
        tangent = jnp.tanh(ROOT * (hidden + CUBIC * square * hidden))
        active = (0.5 * hidden * (1.0 + tangent) * keep).astype(BF16)
        for h in range(2):
            put_part(FWD, h, dot_nn(active, w_out[layer, :, pl.ds(h * HALF, HALF)]))
        slope = 0.5 * (1.0 + tangent) + 0.5 * hidden * (1.0 - tangent * tangent) * ROOT * (
            1.0 + 3.0 * CUBIC * square
        )
        slope_k[...] = slope * keep
        act_t[s] = active.astype(F32).T.astype(BF16)

        gather_wait(BWD, s, 0)
        back = dot_nt(gathered(BWD, s, 0), w_out[layer, :, pl.ds(0, HALF)])
        gather_wait(BWD, s, 1)
        back = back + dot_nt(gathered(BWD, s, 1), w_out[layer, :, pl.ds(HALF, HALF)])
        back_hidden = (back * slope_k[...]).astype(BF16)
        back_h[s] = back_hidden
        for h in range(2):
            put_part(BWD, h, dot_nt(back_hidden, w_in[layer, pl.ds(h * HALF, HALF)]))

        gather_sent(FWD, s)
        gather_sent(BWD, s)
        sum_mid(FWD)
        sum_mid(BWD)

        @pl.when(s >= 2)
        def _():
            for h in range(2):
                cols = pl.ds(h * HALF, HALF)
                g_out = dot_nn(act_t[s - 2], gathered(BWD, s - 2, h)) + dot_nn(act_t[s], gathered(BWD, s, h))
                gw_out[layer, :, cols] = g_out.astype(BF16)
                g_in = dot_tn(gathered(FWD, s - 2, h), back_h[s - 2]) + dot_tn(gathered(FWD, s, h), back_h[s])
                gw_in[layer, cols] = g_in.astype(BF16)
            pltpu.make_async_copy(gw_in.at[layer], grad_in_hbm.at[layer], out_s.at[layer, 0]).start()
            pltpu.make_async_copy(gw_out.at[layer], grad_out_hbm.at[layer], out_s.at[layer, 1]).start()

        sum_end(FWD, k)
        sum_end(BWD, k)

        branch = whole_sum(FWD, k)
        for h in range(2):
            rows[tick, FWD, k + 2, h] = (rows[tick, FWD, k, h].astype(F32) - branch[h]).astype(BF16)

        @pl.when(s == 0)
        def _():
            hand_on(FWD, 0)

        @pl.when(s == 1)
        def _():
            hand_on(FWD, 1)
            take_over(FWD)

        @pl.when(s < 3)
        def _():
            begin(FWD, s + 1)

        back_normed = whole_sum(BWD, k)
        scale, unit = norm_of(tick, k + 1)
        gain = gain_row(layer)
        back_unit = [back_normed[h] * gain[:, h * HALF : (h + 1) * HALF] for h in range(2)]
        mean = (
            jnp.sum(back_unit[0] * unit[0], axis=-1, keepdims=True)
            + jnp.sum(back_unit[1] * unit[1], axis=-1, keepdims=True)
        ) * (1.0 / (2 * HALF))
        for h in range(2):
            back_input = scale * (back_unit[h] - unit[h] * mean)
            rows[tick, BWD, k + 2, h] = (rows[tick, BWD, k, h].astype(F32) + back_input).astype(BF16)

        @pl.when(s == 0)
        def _():
            hand_on(BWD, 0)

        @pl.when(s == 1)
        def _():
            hand_on(BWD, 1)
            take_over(BWD)

        @pl.when(s < 3)
        def _():
            begin(BWD, s + 1)

        for h in range(2):
            term = jnp.sum(back_normed[h] * unit[h], axis=0, keepdims=True)
            gsum[layer, h] += jnp.broadcast_to(term, (8, HALF))
        sum_sent(FWD)
        sum_sent(BWD)
        return carry

    lax.fori_loop(0, 4, step, 0)

    row_id = lax.broadcasted_iota(jnp.int32, (8, HALF), 0)
    mine = jnp.zeros((8, HALF), F32)
    for layer in range(2):
        for h in range(2):
            mine = jnp.where(row_id == 2 * layer + h, gsum[layer, h], mine)
    grx[3] = mine
    for d in (1, 2, 3):
        send(grx.at[3], grx.at[d - 1], gx_s.at[0], gx_r.at[0], x_peer(d))

    for tick in range(2):
        for j, (chain, place) in enumerate(((FWD, 3), (FWD, 2), (BWD, 2), (BWD, 3))):
            for h in range(2):
                v = rows[tick, chain, place, h].astype(F32)
                rebuilt[tick, j, :, h * HALF : (h + 1) * HALF] = jnp.where(z == 0, v[:8], v[8:]).astype(BF16)

    wait(grx.at[pl.ds(0, 3)], gx_r.at[0])
    gry[3] = grx[3] + grx[0] + grx[1] + grx[2]
    for d in (1, 2, 3):
        send(gry.at[3], gry.at[d - 1], gx_s.at[1], gx_r.at[1], y_peer(d))
    wait(gry.at[pl.ds(0, 3)], gx_r.at[1])
    total = gry[3] + gry[0] + gry[1] + gry[2]
    for layer in range(2):
        for h in range(2):
            grad_gains[0, layer : layer + 1, h * HALF : (h + 1) * HALF] = total[2 * layer + h : 2 * layer + h + 1]

    wait(grx.at[pl.ds(0, 3)], gx_s.at[0])
    wait(gry.at[pl.ds(0, 3)], gx_s.at[1])
    for j in range(4):
        wait(hs.at[0, j], hs_s.at[j])

    @pl.when(sec == last)
    def _():
        for j in range(4):
            wait(hs.at[1, j], hs_s.at[4 + j])

    @pl.when(sec > 0)
    def _():
        for chain in range(2):
            for k in range(2):
                wait(rows.at[0, chain, k + 2], tick_s.at[chain, k])

    for layer in range(2):
        pltpu.make_async_copy(gw_in.at[layer], grad_in_hbm.at[layer], out_s.at[layer, 0]).wait()
        pltpu.make_async_copy(gw_out.at[layer], grad_out_hbm.at[layer], out_s.at[layer, 1]).wait()


def per_device(held, head, gains, w_in, w_out, masks):
    vmem = pl.BlockSpec(memory_space=pltpu.VMEM)
    anywhere = pl.BlockSpec(memory_space=pl.ANY)
    dma = pltpu.SemaphoreType.DMA
    rebuilt, grad_in, grad_out, grad_gains = pl.pallas_call(
        kernel,
        out_shape=(
            jax.ShapeDtypeStruct((2, 4, 8, 2 * HALF), BF16),
            jax.ShapeDtypeStruct((2, 2 * HALF, 256), BF16),
            jax.ShapeDtypeStruct((2, 256, 2 * HALF), BF16),
            jax.ShapeDtypeStruct((1, 2, 2 * HALF), F32),
        ),
        in_specs=[vmem, vmem, vmem, anywhere, anywhere, anywhere],
        out_specs=(vmem, anywhere, anywhere, vmem),
        scratch_shapes=[
            pltpu.VMEM((2, 2 * HALF, 256), BF16),
            pltpu.VMEM((2, 256, 2 * HALF), BF16),
            pltpu.VMEM((2, 2, 16, 2, 8, 256), jnp.int32),
            pltpu.VMEM((4, 2, 2, 4, 4, 16, HALF), BF16),
            pltpu.VMEM((2, 2, 4, 4, 16, HALF), BF16),
            pltpu.VMEM((2, 2, 3, 4, 16, HALF), BF16),
            pltpu.VMEM((2, 2, 4, 16, HALF), BF16),
            pltpu.VMEM((2, 2, 3, 16, HALF), BF16),
            pltpu.VMEM((2, 2, 16, HALF), BF16),
            pltpu.VMEM((2, 2, 2, 16, HALF), BF16),
            pltpu.VMEM((2, 2, 4, 2, 16, HALF), BF16),
            pltpu.VMEM((4, 256, 256), BF16),
            pltpu.VMEM((4, 256, 256), BF16),
            pltpu.VMEM((256, 256), F32),
            pltpu.VMEM((2, 2 * HALF, 256), BF16),
            pltpu.VMEM((2, 256, 2 * HALF), BF16),
            pltpu.VMEM((2, 4, 16, HALF), BF16),
            pltpu.VMEM((2, 4, 16, HALF), BF16),
            pltpu.VMEM((2, 2, 8, HALF), F32),
            pltpu.VMEM((4, 8, HALF), F32),
            pltpu.VMEM((4, 8, HALF), F32),
            dma((2, 2)), dma((2, 2)),
            dma((2, 2)), dma((2, 2)),
            dma((2, 2)), dma((2, 2)),
            dma((2, 2)), dma((2, 2)),
            dma((2, 2)), dma((2, 2)),
            dma((2,)), dma((2, 2)),
            dma((2, 2)), dma((2, 2)),
            dma((8,)), dma((8,)),
            dma((2,)), dma((2,)),
            dma((18,)),
            dma((2, 2)),
        ],
        compiler_params=pltpu.CompilerParams(
            collective_id=0, has_side_effects=True, vmem_limit_bytes=52 * 2**20
        ),
        name="relay",
    )(held[0], head, gains, w_in[0], w_out[0], masks.reshape(2, 2, 2, 16, 8, 256))
    return rebuilt[None], grad_in[None], grad_out[None], grad_gains


def solution(mesh):
    return jax.shard_map(
        per_device,
        mesh=mesh,
        in_specs=(
            P("section", None, "tensor", None),
            P(None, "tensor", None),
            P("section", None, None),
            P("section", None, None, "tensor"),
            P("section", None, "tensor", None),
            P("section", None, None, None, "tensor"),
        ),
        out_specs=(
            P("section", None, None, "tensor", None),
            P("section", None, None, "tensor"),
            P("section", None, "tensor", None),
            P("section", None, None),
        ),
        check_vma=False,
    )
```

```python
import math

import jax
import jax.numpy as jnp
from jax import lax
from jax.experimental import pallas as pl
from jax.experimental.pallas import tpu as pltpu
from jax.sharding import PartitionSpec as P

KEEP = 0.9
EPS = 1e-05
CUBIC = 0.044715
ROOT = math.sqrt(2.0 / math.pi)
MESH = pl.DeviceIdType.MESH
F32 = jnp.float32
BF16 = jnp.bfloat16
FWD, BWD = 0, 1
HALF = 1024
QUARTER = 512
OFFSETS = (2, 1, 3)
VMEM_BYTES = 63 * 2**20


def dot_nn(a, b):
    return lax.dot_general(a, b, (((1,), (0,)), ((), ())), preferred_element_type=F32)


def dot_nt(a, b):
    return lax.dot_general(a, b, (((1,), (1,)), ((), ())), preferred_element_type=F32)


def dot_tn(a, b):
    return lax.dot_general(a, b, (((0,), (0,)), ((), ())), preferred_element_type=F32)


def kernel(
    held_hbm, head_hbm, gains_hbm, w_in_hbm, w_out_hbm, masks_hbm,
    rebuilt, grad_in_hbm, grad_out_hbm, grad_gains,
    gw_in, gw_out, held, head, gains, w_in, w_out, masks, gath, part, r1, s1, r2, zs, zr, rf, rows, act_t, back_h, slope_k,
    hs, hr, gain_sum, grx, gry, grz,
    ag1_s, ag1_r, agx_s, agx_r, ag2_s, agf_r, agn_r, agp_s, agp_r,
    rs1_s, rs1_r, rsf_r, rsp_s, rsp_r, rs2_s, rs2_r, z_s, z_r,
    tick_s, tick_r, hs_s, hs_r, gx_s, gx_r, load_s, out_s,
):
    sec = lax.axis_index("section")
    me = lax.axis_index("tensor")
    last = lax.axis_size("section") - 1
    x = lax.rem(me, 4)
    y = lax.rem(me // 4, 4)
    z = me // 16

    def x_peer(d):
        return {"tensor": z * 16 + y * 4 + lax.rem(x + d, 4)}

    def y_peer(d):
        return {"tensor": z * 16 + lax.rem(y + d, 4) * 4 + x}

    z_peer = {"tensor": lax.rem(me + 16, 32)}

    def send(src, dst, s_sem, r_sem, device):
        pltpu.make_async_remote_copy(
            src_ref=src, dst_ref=dst, send_sem=s_sem, recv_sem=r_sem,
            device_id=device, device_id_type=MESH,
        ).start()

    def wait(ref, sem):
        pltpu.make_async_copy(ref, ref, sem).wait()

    first_loads = [
        pltpu.make_async_copy(held_hbm, held, load_s.at[18]),
        pltpu.make_async_copy(head_hbm, head, load_s.at[19]),
        pltpu.make_async_copy(gains_hbm, gains, load_s.at[20]),
    ]
    loads = [
        pltpu.make_async_copy(w_in_hbm, w_in, load_s.at[0]),
        pltpu.make_async_copy(w_out_hbm, w_out, load_s.at[1]),
    ]
    for dy in range(4):
        for dx in range(4):
            block = lax.rem(y + dy, 4) * 4 + lax.rem(x + dx, 4)
            loads.append(
                pltpu.make_async_copy(
                    masks_hbm.at[:, :, :, block], masks.at[:, :, dy * 4 + dx], load_s.at[2 + dy * 4 + dx]
                )
            )
    for copy in first_loads + loads:
        copy.start()

    barrier = pltpu.get_barrier_semaphore()
    for d in (1, 2, 3):
        pl.semaphore_signal(barrier, inc=1, device_id=x_peer(d), device_id_type=MESH)
        pl.semaphore_signal(barrier, inc=1, device_id=y_peer(d), device_id_type=MESH)
    pl.semaphore_signal(barrier, inc=1, device_id=z_peer, device_id_type=MESH)

    above = {"section": lax.rem(sec + 1, last + 1)}
    pl.semaphore_signal(barrier, inc=1, device_id=above, device_id_type=MESH)

    def pack(source, slot):
        for j in range(4):
            v = source[j].astype(F32)
            hs[slot, j] = jnp.concatenate([v[:, :HALF], v[:, HALF:]], axis=0).astype(BF16)

    for copy in first_loads:
        copy.wait()
    pack(held, 0)

    pl.semaphore_wait(barrier, 8)

    places = ((0, FWD, 1), (3, BWD, 1), (1, FWD, 0), (2, BWD, 0))
    for j, _, _ in places:
        send(hs.at[0, j], hr.at[0, j], hs_s.at[j], hs_r.at[j], z_peer)

    @pl.when(sec == last)
    def _():
        pack(head, 1)
        for j, _, _ in places:
            send(hs.at[1, j], hr.at[1, j], hs_s.at[4 + j], hs_r.at[4 + j], z_peer)

    def unpack(slot, j, tick, chain, place):
        wait(hr.at[slot, j], hs_r.at[4 * slot + j])
        mine = hs[slot, j].astype(F32)
        theirs = hr[slot, j].astype(F32)
        for h in range(2):
            a = mine[8 * h : 8 * h + 8]
            b = theirs[8 * h : 8 * h + 8]
            both = jnp.concatenate([jnp.where(z == 0, a, b), jnp.where(z == 0, b, a)], axis=0)
            rows[tick, chain, place, h] = both.astype(BF16)

    def gain_row(layer):
        pair = gains[0]
        return jnp.where(layer == 1, pair[1:2], pair[0:1])

    def norm_of(tick, place):
        v0 = rows[tick, FWD, place, 0].astype(F32)
        v1 = rows[tick, FWD, place, 1].astype(F32)
        total = jnp.sum(v0 * v0, axis=-1, keepdims=True) + jnp.sum(v1 * v1, axis=-1, keepdims=True)
        scale = lax.rsqrt(total * (1.0 / (2 * HALF)) + EPS)
        return scale, (v0 * scale, v1 * scale)

    def gather_start(chain, s):
        for d in OFFSETS:
            send(gath.at[s, chain, 0, 0, 0], gath.at[s, chain, 0, 0, 4 - d], ag1_s.at[chain, 0], ag1_r.at[chain, 0], x_peer(d))
            send(gath.at[s, chain, 1, 0, 0], gath.at[s, chain, 1, 4 - d, 0], ag1_s.at[chain, 1], ag1_r.at[chain, 1], y_peer(d))
        for d in OFFSETS:
            send(gath.at[s, chain, 0, 0, 0], gath.at[s, chain, 0, 4 - d, 0], agx_s.at[chain, 0], agx_r.at[chain, 0], y_peer(d))
            send(gath.at[s, chain, 1, 0, 0], gath.at[s, chain, 1, 0, 4 - d], agx_s.at[chain, 1], agx_r.at[chain, 1], x_peer(d))

    def second_axis(h):
        return y_peer if h == 0 else x_peer

    def blocks(chain, s, h, place, q):
        cols = pl.ds(q * QUARTER, QUARTER)
        if h == 0:
            return gath.at[s, chain, 0, place, pl.ds(1, 3), :, cols]
        return gath.at[s, chain, 1, pl.ds(1, 3), place, :, cols]

    def three(chain, s, h):
        return gath.at[s, chain, h, 0, pl.ds(1, 3)]

    def gather_mid(chain, s):
        for h in range(2):
            wait(three(chain, s, h), ag1_r.at[chain, h])
        for q in range(2):
            for h in range(2):
                peer = second_axis(h)
                for right in range(2):
                    cols = q if right else 1 - q
                    r_sem = agf_r.at[chain, h, right] if q == 0 else agn_r.at[chain, h]
                    send(
                        blocks(chain, s, h, 0, cols), blocks(chain, s, h, 3 if right else 1, cols),
                        ag2_s.at[chain, h], r_sem, peer(1 if right else 3),
                    )

    def gather_pass(chain, s):
        for right in (1, 0):
            for h in range(2):
                cols = 0 if right else 1
                came = blocks(chain, s, h, 3 if right else 1, cols)
                wait(came, agf_r.at[chain, h, right])
                send(
                    came, blocks(chain, s, h, 2, cols), agp_s.at[chain, h], agp_r.at[chain, h],
                    second_axis(h)(1 if right else 3),
                )

    def gather_wait(chain, s, h):
        wait(three(chain, s, h), agx_r.at[chain, h])
        wait(three(chain, s, h), agn_r.at[chain, h])
        wait(three(chain, s, h), agp_r.at[chain, h])

    def gather_sent(chain, s):
        for h in range(2):
            wait(three(chain, s, h), ag1_s.at[chain, h])
            wait(three(chain, s, h), agx_s.at[chain, h])
            wait(gath.at[s, chain, h, pl.ds(0, 2), pl.ds(1, 3)], ag2_s.at[chain, h])
            wait(three(chain, s, h), agp_s.at[chain, h])

    def gathered(chain, s, h):
        return gath[s, chain, h].reshape(256, HALF)

    def first_axis(h):
        return x_peer if h == 0 else y_peer

    def strip(chain, h, d, q):
        cols = pl.ds(q * QUARTER, QUARTER)
        if h == 0:
            return part.at[chain, 0, :, d, :, cols]
        return part.at[chain, 1, d, :, :, cols]

    def put_part(chain, h, value):
        part[chain, h] = value.astype(BF16).reshape(4, 4, 16, HALF)
        peer = first_axis(h)
        for right in (1, 0):
            send(
                strip(chain, h, 2, 1 - right), rf.at[chain, h, right],
                rs1_s.at[chain, h], rsf_r.at[chain, h, right], peer(1 if right else 3),
            )
        for right in (1, 0):
            send(
                strip(chain, h, 1 if right else 3, right), r1.at[chain, h, right, :, :, pl.ds(right * QUARTER, QUARTER)],
                rs1_s.at[chain, h], rs1_r.at[chain, h], peer(1 if right else 3),
            )

    def sum_pass(chain):
        for right in (1, 0):
            for h in range(2):
                d, q = (1, 0) if right else (3, 1)
                wait(rf.at[chain, h, right], rsf_r.at[chain, h, right])
                own = strip(chain, h, d, q)
                own[...] = (own[...].astype(F32) + rf[chain, h, right].astype(F32)).astype(BF16)
                send(
                    own, r1.at[chain, h, right, :, :, pl.ds(q * QUARTER, QUARTER)],
                    rsp_s.at[chain, h], rsp_r.at[chain, h], first_axis(h)(1 if right else 3),
                )

    def sum_mid(chain):
        for h in range(2):
            wait(r1.at[chain, h, 0], rs1_r.at[chain, h])
            wait(r1.at[chain, h, 0], rsp_r.at[chain, h])
            for d in OFFSETS + (0,):
                own = part[chain, 0, d, 0] if h == 0 else part[chain, 1, 0, d]
                total = own.astype(F32) + (r1[chain, h, 0, d].astype(F32) + r1[chain, h, 1, d].astype(F32))
                s1[chain, h, d] = total.astype(BF16)
                if d:
                    send(
                        s1.at[chain, h, d], r2.at[chain, h, d - 1], rs2_s.at[chain, h], rs2_r.at[chain, h],
                        y_peer(d) if h == 0 else x_peer(d),
                    )

    def sum_end(chain, k):
        for h in range(2):
            wait(r2.at[chain, h], rs2_r.at[chain, h])
            total = s1[chain, h, 0].astype(F32)
            for j in range(3):
                total = total + r2[chain, h, j].astype(F32)
            zs[chain, h] = total.astype(BF16)
        send(zs.at[chain], zr.at[k, chain], z_s.at[chain], z_r.at[k, chain], z_peer)

    def sum_sent(chain):
        for h in range(2):
            wait(r1.at[chain, h], rs1_s.at[chain, h])
            wait(r1.at[chain, h, 0], rsp_s.at[chain, h])
            wait(r2.at[chain, h], rs2_s.at[chain, h])
        wait(zs.at[chain], z_s.at[chain])

    def whole_sum(chain, k):
        wait(zr.at[k, chain], z_r.at[k, chain])
        return [zs[chain, h].astype(F32) + zr[k, chain, h].astype(F32) for h in range(2)]

    def begin(chain, s):
        tick, k = s // 2, lax.rem(s, 2)
        if chain == FWD:
            gain = gain_row(1 - k)
            _, unit = norm_of(tick, k + 1)
            for h in range(2):
                gath[s, FWD, h, 0, 0] = (unit[h] * gain[:, h * HALF : (h + 1) * HALF]).astype(BF16)
        else:
            for h in range(2):
                gath[s, BWD, h, 0, 0] = rows[tick, BWD, k + 1, h]
        gather_start(chain, s)

    def hand_on(chain, k):
        @pl.when(sec > 0)
        def _():
            send(
                rows.at[0, chain, k + 2], rows.at[1, chain, k], tick_s.at[chain, k], tick_r.at[chain, k],
                {"section": sec - 1},
            )

    def take_over(chain):
        @pl.when(sec < last)
        def _():
            for k in range(2):
                wait(rows.at[1, chain, k], tick_r.at[chain, k])

    for j, chain, place in places[:2]:
        unpack(0, j, 0, chain, place)
        begin(chain, 0)
    for j, chain, place in places[2:]:
        unpack(0, j, 0, chain, place)

    @pl.when(sec == last)
    def _():
        for j, chain, place in places:
            unpack(1, j, 1, chain, place)

    for copy in loads:
        copy.wait()

    def forward(s):
        tick, k = s // 2, lax.rem(s, 2)
        layer = 1 - k
        gather_wait(FWD, s, 0)
        hidden = dot_nn(gathered(FWD, s, 0), w_in[layer, pl.ds(0, HALF)])
        gather_wait(FWD, s, 1)
        hidden = hidden + dot_nn(gathered(FWD, s, 1), w_in[layer, pl.ds(HALF, HALF)])
        keep = masks[tick, layer].reshape(256, 256).astype(F32) * (1.0 / KEEP)
        square = hidden * hidden
        tangent = jnp.tanh(ROOT * (hidden + CUBIC * square * hidden))
        active = (0.5 * hidden * (1.0 + tangent) * keep).astype(BF16)
        for h in range(2):
            put_part(FWD, h, dot_nn(active, w_out[layer, :, pl.ds(h * HALF, HALF)]))
        slope = 0.5 * (1.0 + tangent) + 0.5 * hidden * (1.0 - tangent * tangent) * ROOT * (
            1.0 + 3.0 * CUBIC * square
        )
        slope_k[...] = slope * keep
        act_t[s] = active.astype(F32).T.astype(BF16)

    def backward(s):
        layer = 1 - lax.rem(s, 2)
        gather_wait(BWD, s, 0)
        back = dot_nt(gathered(BWD, s, 0), w_out[layer, :, pl.ds(0, HALF)])
        gather_wait(BWD, s, 1)
        back = back + dot_nt(gathered(BWD, s, 1), w_out[layer, :, pl.ds(HALF, HALF)])
        back_hidden = (back * slope_k[...]).astype(BF16)
        back_h[s] = back_hidden
        for h in range(2):
            put_part(BWD, h, dot_nt(back_hidden, w_in[layer, pl.ds(h * HALF, HALF)]))

    def forward_rows(s):
        tick, k = s // 2, lax.rem(s, 2)
        branch = whole_sum(FWD, k)
        for h in range(2):
            rows[tick, FWD, k + 2, h] = (rows[tick, FWD, k, h].astype(F32) - branch[h]).astype(BF16)

    def backward_rows(s):
        tick, k = s // 2, lax.rem(s, 2)
        scale, unit = norm_of(tick, k + 1)
        gain = gain_row(1 - k)
        back_normed = whole_sum(BWD, k)
        back_unit = [back_normed[h] * gain[:, h * HALF : (h + 1) * HALF] for h in range(2)]
        mean = (
            jnp.sum(back_unit[0] * unit[0], axis=-1, keepdims=True)
            + jnp.sum(back_unit[1] * unit[1], axis=-1, keepdims=True)
        ) * (1.0 / (2 * HALF))
        for h in range(2):
            back_input = scale * (back_unit[h] - unit[h] * mean)
            rows[tick, BWD, k + 2, h] = (rows[tick, BWD, k, h].astype(F32) + back_input).astype(BF16)

    def next_rows(chain, s):
        @pl.when(s == 0)
        def _():
            hand_on(chain, 0)

        @pl.when(s == 1)
        def _():
            hand_on(chain, 1)
            take_over(chain)

        @pl.when(s < 3)
        def _():
            begin(chain, s + 1)

    def grad_out(layer):
        for h in range(2):
            first, second = 1 - layer, 3 - layer
            g_out = dot_nn(act_t[first], gathered(BWD, first, h)) + dot_nn(act_t[second], gathered(BWD, second, h))
            gw_out[layer, :, pl.ds(h * HALF, HALF)] = g_out.astype(BF16)

    def grad_in(layer):
        for h in range(2):
            first, second = 1 - layer, 3 - layer
            span = pl.ds(h * HALF, HALF)
            g_in = dot_tn(gathered(FWD, first, h), back_h[first]) + dot_tn(gathered(FWD, second, h), back_h[second])
            gw_in[layer, span] = g_in.astype(BF16)
            product = (g_in * w_in[layer, span].astype(F32)).astype(BF16)
            sums = dot_nt(jnp.ones((8, 256), BF16), product)
            gain_sum[2 * layer + h] = sums / gains[0, layer : layer + 1, h * HALF : (h + 1) * HALF]

    def out_copy(layer, which):
        if which == 0:
            return pltpu.make_async_copy(gw_in.at[layer], grad_in_hbm.at[layer], out_s.at[layer, 0])
        return pltpu.make_async_copy(gw_out.at[layer], grad_out_hbm.at[layer], out_s.at[layer, 1])

    def put_rows(tick, j):
        chain, place = ((FWD, 3), (FWD, 2), (BWD, 2), (BWD, 3))[j]
        for h in range(2):
            v = rows[tick, chain, place, h].astype(F32)
            rebuilt[tick, j, :, h * HALF : (h + 1) * HALF] = jnp.where(z == 0, v[:8], v[8:]).astype(BF16)

    def while_first_sum():
        for layer in (1, 0):
            grad_in(layer)
            out_copy(layer, 0).start()
        mine = [gain_sum[j, 0:1] for j in range(4)]
        grx[x] = jnp.concatenate(mine + mine, axis=0)
        for d in (1, 2, 3):
            send(grx.at[x], grx.at[x], gx_s.at[0], gx_r.at[0], x_peer(d))

    def while_second_sum():
        wait(grx.at[pl.ds(0, 3)], gx_r.at[0])
        gry[y] = (grx[0] + grx[1]) + (grx[2] + grx[3])
        for d in (1, 2, 3):
            send(gry.at[y], gry.at[y], gx_s.at[1], gx_r.at[1], y_peer(d))
        for layer in (1, 0):
            grad_out(layer)
            out_copy(layer, 1).start()

    def while_third_sum():
        wait(gry.at[pl.ds(0, 3)], gx_r.at[1])
        grz[0] = (gry[0] + gry[1]) + (gry[2] + gry[3])
        send(grz.at[0], grz.at[1], gx_s.at[2], gx_r.at[2], z_peer)
        for j in range(4):
            put_rows(0, j)
        put_rows(1, 1)
        put_rows(1, 2)

    def step(s, carry):
        k = lax.rem(s, 2)
        gather_mid(FWD, s)
        gather_mid(BWD, s)
        gather_pass(FWD, s)
        gather_pass(BWD, s)
        forward(s)
        backward(s)
        sum_pass(FWD)
        sum_pass(BWD)
        pl.when(s == 3)(while_first_sum)
        gather_sent(FWD, s)
        gather_sent(BWD, s)
        sum_mid(FWD)
        sum_mid(BWD)
        pl.when(s == 3)(while_second_sum)
        sum_end(FWD, k)
        sum_end(BWD, k)
        pl.when(s == 3)(while_third_sum)
        forward_rows(s)
        next_rows(FWD, s)
        backward_rows(s)
        next_rows(BWD, s)
        sum_sent(FWD)
        sum_sent(BWD)
        return carry

    lax.fori_loop(0, 4, step, 0)

    put_rows(1, 0)
    put_rows(1, 3)
    wait(grz.at[1], gx_r.at[2])
    total = grz[0] + grz[1]
    for layer in range(2):
        for h in range(2):
            grad_gains[0, layer : layer + 1, h * HALF : (h + 1) * HALF] = total[2 * layer + h : 2 * layer + h + 1]

    wait(grx.at[pl.ds(0, 3)], gx_s.at[0])
    wait(gry.at[pl.ds(0, 3)], gx_s.at[1])
    wait(grz.at[0], gx_s.at[2])
    for j in range(4):
        wait(hs.at[0, j], hs_s.at[j])

    @pl.when(sec == last)
    def _():
        for j in range(4):
            wait(hs.at[1, j], hs_s.at[4 + j])

    @pl.when(sec > 0)
    def _():
        for chain in range(2):
            for k in range(2):
                wait(rows.at[0, chain, k + 2], tick_s.at[chain, k])

    for layer in range(2):
        for which in range(2):
            out_copy(layer, which).wait()


def write_out(*refs):
    sources, results, held, sems = refs[:4], refs[4:8], refs[8:12], refs[12]

    def pieces(first, second):
        found = [(0, ...), (3, ...)]
        for layer in range(2):
            for j in range(4):
                found.append((1, (layer, pl.ds(512 * j, 512))))
                found.append((2, (layer, pl.ds(64 * j, 64))))
        return [
            pltpu.make_async_copy(first[i].at[at], second[i].at[at], sems.at[n, 0 if second is held else 1])
            for n, (i, at) in enumerate(found)
        ]

    loads, stores = pieces(sources, held), pieces(held, results)
    for load in loads:
        load.start()
    for load, store in zip(loads, stores):
        load.wait()
        store.start()
    for store in stores:
        store.wait()


def per_device(held, head, gains, w_in, w_out, masks):
    vmem = pl.BlockSpec(memory_space=pltpu.VMEM)
    anywhere = pl.BlockSpec(memory_space=pl.ANY)
    dma = pltpu.SemaphoreType.DMA
    shapes = (
        jax.ShapeDtypeStruct((2, 4, 8, 2 * HALF), BF16),
        jax.ShapeDtypeStruct((2, 2 * HALF, 256), BF16),
        jax.ShapeDtypeStruct((2, 256, 2 * HALF), BF16),
        jax.ShapeDtypeStruct((1, 2, 2 * HALF), F32),
    )
    results = pl.pallas_call(
        kernel,
        out_shape=shapes,
        in_specs=[anywhere] * 6,
        out_specs=(vmem, anywhere, anywhere, vmem),
        scratch_shapes=[
            pltpu.VMEM((2, 2 * HALF, 256), BF16),
            pltpu.VMEM((2, 256, 2 * HALF), BF16),
            pltpu.VMEM((4, 8, 2 * HALF), BF16),
            pltpu.VMEM((4, 8, 2 * HALF), BF16),
            pltpu.VMEM((1, 2, 2 * HALF), F32),
            pltpu.VMEM((2, 2 * HALF, 256), BF16),
            pltpu.VMEM((2, 256, 2 * HALF), BF16),
            pltpu.VMEM((2, 2, 16, 2, 8, 256), jnp.int32),
            pltpu.VMEM((4, 2, 2, 4, 4, 16, HALF), BF16),
            pltpu.VMEM((2, 2, 4, 4, 16, HALF), BF16),
            pltpu.VMEM((2, 2, 2, 4, 16, HALF), BF16),
            pltpu.VMEM((2, 2, 4, 16, HALF), BF16),
            pltpu.VMEM((2, 2, 3, 16, HALF), BF16),
            pltpu.VMEM((2, 2, 16, HALF), BF16),
            pltpu.VMEM((2, 2, 2, 16, HALF), BF16),
            pltpu.VMEM((2, 2, 2, 4, 16, QUARTER), BF16),
            pltpu.VMEM((2, 2, 4, 2, 16, HALF), BF16),
            pltpu.VMEM((4, 256, 256), BF16),
            pltpu.VMEM((4, 256, 256), BF16),
            pltpu.VMEM((256, 256), F32),
            pltpu.VMEM((2, 4, 16, HALF), BF16),
            pltpu.VMEM((2, 4, 16, HALF), BF16),
            pltpu.VMEM((4, 8, HALF), F32),
            pltpu.VMEM((4, 8, HALF), F32),
            pltpu.VMEM((4, 8, HALF), F32),
            pltpu.VMEM((2, 8, HALF), F32),
            dma((2, 2)), dma((2, 2)),
            dma((2, 2)), dma((2, 2)),
            dma((2, 2)), dma((2, 2, 2)), dma((2, 2)), dma((2, 2)), dma((2, 2)),
            dma((2, 2)), dma((2, 2)), dma((2, 2, 2)), dma((2, 2)), dma((2, 2)),
            dma((2, 2)), dma((2, 2)),
            dma((2,)), dma((2, 2)),
            dma((2, 2)), dma((2, 2)),
            dma((8,)), dma((8,)),
            dma((3,)), dma((3,)),
            dma((21,)),
            dma((2, 2)),
        ],
        compiler_params=pltpu.CompilerParams(
            collective_id=0, has_side_effects=True, vmem_limit_bytes=VMEM_BYTES
        ),
        name="relay",
    )(held[0], head, gains, w_in[0], w_out[0], masks.reshape(2, 2, 2, 16, 8, 256))
    rebuilt, grad_in, grad_out, grad_gains = pl.pallas_call(
        write_out,
        out_shape=shapes,
        in_specs=[anywhere] * 4,
        out_specs=(anywhere,) * 4,
        scratch_shapes=[pltpu.VMEM(shape.shape, shape.dtype) for shape in shapes] + [dma((18, 2))],
        compiler_params=pltpu.CompilerParams(vmem_limit_bytes=VMEM_BYTES),
        name="write_out",
    )(*results)
    return rebuilt[None], grad_in[None], grad_out[None], grad_gains


def solution(mesh):
    return jax.shard_map(
        per_device,
        mesh=mesh,
        in_specs=(
            P("section", None, "tensor", None),
            P(None, "tensor", None),
            P("section", None, None),
            P("section", None, None, "tensor"),
            P("section", None, "tensor", None),
            P("section", None, None, None, "tensor"),
        ),
        out_specs=(
            P("section", None, None, "tensor", None),
            P("section", None, None, "tensor"),
            P("section", None, "tensor", None),
            P("section", None, None),
        ),
        check_vma=False,
    )
```

```python
import math

import jax
import jax.numpy as jnp
from jax import lax
from jax.experimental import pallas as pl
from jax.experimental.pallas import tpu as pltpu
from jax.sharding import PartitionSpec as P

KEEP = 0.9
EPS = 1e-05
CUBIC = 0.044715
ROOT = math.sqrt(2.0 / math.pi)
MESH = pl.DeviceIdType.MESH
F32 = jnp.float32
BF16 = jnp.bfloat16
FWD, BWD = 0, 1
HALF = 1024
QUARTER = 512
OFFSETS = (2, 1, 3)
VMEM_BYTES = 63 * 2**20


def dot_nn(a, b):
    return lax.dot_general(a, b, (((1,), (0,)), ((), ())), preferred_element_type=F32)


def dot_nt(a, b):
    return lax.dot_general(a, b, (((1,), (1,)), ((), ())), preferred_element_type=F32)


def dot_tn(a, b):
    return lax.dot_general(a, b, (((0,), (0,)), ((), ())), preferred_element_type=F32)


def kernel(
    held_hbm, head_hbm, gains_hbm, w_in_hbm, w_out_hbm, masks_hbm,
    rebuilt, grad_in_hbm, grad_out_hbm, grad_gains,
    gw_in, gw_out, held, head, gains, w_in, w_out, masks, gath, part, r1, s1, r2, zs, zr, rf, rows, act_t, back_h, slope_k,
    hs, hr, gain_sum, grx, gry, grz,
    ag1_s, ag1_r, agx_s, agx_r, ag2_s, agf_r, agn_r, agp_s, agp_r,
    rs1_s, rs1_r, rsf_r, rsp_s, rsp_r, rs2_s, rs2_r, z_s, z_r,
    tick_s, tick_r, hs_s, hs_r, gx_s, gx_r, load_s, out_s,
):
    sec = lax.axis_index("section")
    me = lax.axis_index("tensor")
    last = lax.axis_size("section") - 1
    x = lax.rem(me, 4)
    y = lax.rem(me // 4, 4)
    z = me // 16

    def x_peer(d):
        return {"tensor": z * 16 + y * 4 + lax.rem(x + d, 4)}

    def y_peer(d):
        return {"tensor": z * 16 + lax.rem(y + d, 4) * 4 + x}

    z_peer = {"tensor": lax.rem(me + 16, 32)}

    def send(src, dst, s_sem, r_sem, device):
        pltpu.make_async_remote_copy(
            src_ref=src, dst_ref=dst, send_sem=s_sem, recv_sem=r_sem,
            device_id=device, device_id_type=MESH,
        ).start()

    def wait(ref, sem):
        pltpu.make_async_copy(ref, ref, sem).wait()

    first_loads = [
        pltpu.make_async_copy(held_hbm, held, load_s.at[18]),
        pltpu.make_async_copy(head_hbm, head, load_s.at[19]),
        pltpu.make_async_copy(gains_hbm, gains, load_s.at[20]),
    ]
    loads = [
        pltpu.make_async_copy(w_in_hbm, w_in, load_s.at[0]),
        pltpu.make_async_copy(w_out_hbm, w_out, load_s.at[1]),
    ]
    for dy in range(4):
        for dx in range(4):
            block = lax.rem(y + dy, 4) * 4 + lax.rem(x + dx, 4)
            loads.append(
                pltpu.make_async_copy(
                    masks_hbm.at[:, :, :, block], masks.at[:, :, dy * 4 + dx], load_s.at[2 + dy * 4 + dx]
                )
            )
    for copy in first_loads + loads:
        copy.start()

    barrier = pltpu.get_barrier_semaphore()
    for d in (1, 2, 3):
        pl.semaphore_signal(barrier, inc=1, device_id=x_peer(d), device_id_type=MESH)
        pl.semaphore_signal(barrier, inc=1, device_id=y_peer(d), device_id_type=MESH)
    pl.semaphore_signal(barrier, inc=1, device_id=z_peer, device_id_type=MESH)

    above = {"section": lax.rem(sec + 1, last + 1)}
    pl.semaphore_signal(barrier, inc=1, device_id=above, device_id_type=MESH)

    def pack(source, slot):
        for j in range(4):
            v = source[j].astype(F32)
            hs[slot, j] = jnp.concatenate([v[:, :HALF], v[:, HALF:]], axis=0).astype(BF16)

    for copy in first_loads:
        copy.wait()
    pack(held, 0)

    pl.semaphore_wait(barrier, 8)

    places = ((0, FWD, 1), (3, BWD, 1), (1, FWD, 0), (2, BWD, 0))
    for j, _, _ in places:
        send(hs.at[0, j], hr.at[0, j], hs_s.at[j], hs_r.at[j], z_peer)

    @pl.when(sec == last)
    def _():
        pack(head, 1)
        for j, _, _ in places:
            send(hs.at[1, j], hr.at[1, j], hs_s.at[4 + j], hs_r.at[4 + j], z_peer)

    def unpack(slot, j, tick, chain, place):
        wait(hr.at[slot, j], hs_r.at[4 * slot + j])
        mine = hs[slot, j].astype(F32)
        theirs = hr[slot, j].astype(F32)
        for h in range(2):
            a = mine[8 * h : 8 * h + 8]
            b = theirs[8 * h : 8 * h + 8]
            both = jnp.concatenate([jnp.where(z == 0, a, b), jnp.where(z == 0, b, a)], axis=0)
            rows[tick, chain, place, h] = both.astype(BF16)

    def gain_row(layer):
        pair = gains[0]
        return jnp.where(layer == 1, pair[1:2], pair[0:1])

    def norm_of(tick, place):
        v0 = rows[tick, FWD, place, 0].astype(F32)
        v1 = rows[tick, FWD, place, 1].astype(F32)
        total = jnp.sum(v0 * v0, axis=-1, keepdims=True) + jnp.sum(v1 * v1, axis=-1, keepdims=True)
        scale = lax.rsqrt(total * (1.0 / (2 * HALF)) + EPS)
        return scale, (v0 * scale, v1 * scale)

    def gather_start(chain, s):
        for d in OFFSETS:
            send(gath.at[s, chain, 0, 0, 0], gath.at[s, chain, 0, 0, 4 - d], ag1_s.at[chain, 0], ag1_r.at[chain, 0], x_peer(d))
            send(gath.at[s, chain, 1, 0, 0], gath.at[s, chain, 1, 4 - d, 0], ag1_s.at[chain, 1], ag1_r.at[chain, 1], y_peer(d))
        for d in OFFSETS:
            send(gath.at[s, chain, 0, 0, 0], gath.at[s, chain, 0, 4 - d, 0], agx_s.at[chain, 0], agx_r.at[chain, 0], y_peer(d))
            send(gath.at[s, chain, 1, 0, 0], gath.at[s, chain, 1, 0, 4 - d], agx_s.at[chain, 1], agx_r.at[chain, 1], x_peer(d))

    def second_axis(h):
        return y_peer if h == 0 else x_peer

    def blocks(chain, s, h, place, q):
        cols = pl.ds(q * QUARTER, QUARTER)
        if h == 0:
            return gath.at[s, chain, 0, place, pl.ds(1, 3), :, cols]
        return gath.at[s, chain, 1, pl.ds(1, 3), place, :, cols]

    def three(chain, s, h):
        return gath.at[s, chain, h, 0, pl.ds(1, 3)]

    def gather_mid(chain, s):
        for h in range(2):
            wait(three(chain, s, h), ag1_r.at[chain, h])
        for q in range(2):
            for h in range(2):
                peer = second_axis(h)
                for right in range(2):
                    cols = q if right else 1 - q
                    r_sem = agf_r.at[chain, h, right] if q == 0 else agn_r.at[chain, h]
                    send(
                        blocks(chain, s, h, 0, cols), blocks(chain, s, h, 3 if right else 1, cols),
                        ag2_s.at[chain, h], r_sem, peer(1 if right else 3),
                    )

    def gather_pass(chain, s):
        for right in (1, 0):
            for h in range(2):
                cols = 0 if right else 1
                came = blocks(chain, s, h, 3 if right else 1, cols)
                wait(came, agf_r.at[chain, h, right])
                send(
                    came, blocks(chain, s, h, 2, cols), agp_s.at[chain, h], agp_r.at[chain, h],
                    second_axis(h)(1 if right else 3),
                )

    def gather_wait(chain, s, h):
        wait(three(chain, s, h), agx_r.at[chain, h])
        wait(three(chain, s, h), agn_r.at[chain, h])
        wait(three(chain, s, h), agp_r.at[chain, h])

    def gather_sent(chain, s):
        for h in range(2):
            wait(three(chain, s, h), ag1_s.at[chain, h])
            wait(three(chain, s, h), agx_s.at[chain, h])
            wait(gath.at[s, chain, h, pl.ds(0, 2), pl.ds(1, 3)], ag2_s.at[chain, h])
            wait(three(chain, s, h), agp_s.at[chain, h])

    def gathered(chain, s, h):
        return gath[s, chain, h].reshape(256, HALF)

    def first_axis(h):
        return x_peer if h == 0 else y_peer

    def strip(chain, h, d, q):
        cols = pl.ds(q * QUARTER, QUARTER)
        if h == 0:
            return part.at[chain, 0, :, d, :, cols]
        return part.at[chain, 1, d, :, :, cols]

    def put_part(chain, h, value):
        part[chain, h] = value.astype(BF16).reshape(4, 4, 16, HALF)
        peer = first_axis(h)
        for right in (1, 0):
            send(
                strip(chain, h, 2, 1 - right), rf.at[chain, h, right],
                rs1_s.at[chain, h], rsf_r.at[chain, h, right], peer(1 if right else 3),
            )
        for right in (1, 0):
            send(
                strip(chain, h, 1 if right else 3, right), r1.at[chain, h, right, :, :, pl.ds(right * QUARTER, QUARTER)],
                rs1_s.at[chain, h], rs1_r.at[chain, h], peer(1 if right else 3),
            )

    def sum_pass(chain):
        for right in (1, 0):
            for h in range(2):
                d, q = (1, 0) if right else (3, 1)
                wait(rf.at[chain, h, right], rsf_r.at[chain, h, right])
                own = strip(chain, h, d, q)
                own[...] = (own[...].astype(F32) + rf[chain, h, right].astype(F32)).astype(BF16)
                send(
                    own, r1.at[chain, h, right, :, :, pl.ds(q * QUARTER, QUARTER)],
                    rsp_s.at[chain, h], rsp_r.at[chain, h], first_axis(h)(1 if right else 3),
                )

    def sum_mid(chain):
        for h in range(2):
            wait(r1.at[chain, h, 0], rs1_r.at[chain, h])
            wait(r1.at[chain, h, 0], rsp_r.at[chain, h])
            for d in OFFSETS + (0,):
                own = part[chain, 0, d, 0] if h == 0 else part[chain, 1, 0, d]
                total = own.astype(F32) + (r1[chain, h, 0, d].astype(F32) + r1[chain, h, 1, d].astype(F32))
                s1[chain, h, d] = total.astype(BF16)
                if d:
                    send(
                        s1.at[chain, h, d], r2.at[chain, h, d - 1], rs2_s.at[chain, h], rs2_r.at[chain, h],
                        y_peer(d) if h == 0 else x_peer(d),
                    )

    def sum_end(chain, k):
        for h in range(2):
            wait(r2.at[chain, h], rs2_r.at[chain, h])
            total = s1[chain, h, 0].astype(F32)
            for j in range(3):
                total = total + r2[chain, h, j].astype(F32)
            zs[chain, h] = total.astype(BF16)
            send(zs.at[chain, h], zr.at[k, chain, h], z_s.at[chain], z_r.at[k, chain], z_peer)

    def sum_sent(chain):
        for h in range(2):
            wait(r1.at[chain, h], rs1_s.at[chain, h])
            wait(r1.at[chain, h, 0], rsp_s.at[chain, h])
            wait(r2.at[chain, h], rs2_s.at[chain, h])
        wait(zs.at[chain], z_s.at[chain])

    def whole_sum(chain, k):
        wait(zr.at[k, chain], z_r.at[k, chain])
        return [zs[chain, h].astype(F32) + zr[k, chain, h].astype(F32) for h in range(2)]

    def begin(chain, s):
        tick, k = s // 2, lax.rem(s, 2)
        if chain == FWD:
            gain = gain_row(1 - k)
            _, unit = norm_of(tick, k + 1)
            for h in range(2):
                gath[s, FWD, h, 0, 0] = (unit[h] * gain[:, h * HALF : (h + 1) * HALF]).astype(BF16)
        else:
            for h in range(2):
                gath[s, BWD, h, 0, 0] = rows[tick, BWD, k + 1, h]
        gather_start(chain, s)

    def hand_on(chain, k):
        @pl.when(sec > 0)
        def _():
            send(
                rows.at[0, chain, k + 2], rows.at[1, chain, k], tick_s.at[chain, k], tick_r.at[chain, k],
                {"section": sec - 1},
            )

    def take_over(chain):
        @pl.when(sec < last)
        def _():
            for k in range(2):
                wait(rows.at[1, chain, k], tick_r.at[chain, k])

    for j, chain, place in places[:2]:
        unpack(0, j, 0, chain, place)
        begin(chain, 0)
    for j, chain, place in places[2:]:
        unpack(0, j, 0, chain, place)

    @pl.when(sec == last)
    def _():
        for j, chain, place in places:
            unpack(1, j, 1, chain, place)

    for copy in loads:
        copy.wait()

    def forward(s):
        tick, k = s // 2, lax.rem(s, 2)
        layer = 1 - k
        gather_wait(FWD, s, 0)
        hidden = dot_nn(gathered(FWD, s, 0), w_in[layer, pl.ds(0, HALF)])
        gather_wait(FWD, s, 1)
        hidden = hidden + dot_nn(gathered(FWD, s, 1), w_in[layer, pl.ds(HALF, HALF)])
        keep = masks[tick, layer].reshape(256, 256).astype(F32) * (1.0 / KEEP)
        square = hidden * hidden
        tangent = jnp.tanh(ROOT * (hidden + CUBIC * square * hidden))
        active = (0.5 * hidden * (1.0 + tangent) * keep).astype(BF16)
        for h in range(2):
            put_part(FWD, h, dot_nn(active, w_out[layer, :, pl.ds(h * HALF, HALF)]))
        slope = 0.5 * (1.0 + tangent) + 0.5 * hidden * (1.0 - tangent * tangent) * ROOT * (
            1.0 + 3.0 * CUBIC * square
        )
        slope_k[...] = slope * keep
        act_t[s] = active.astype(F32).T.astype(BF16)

    def backward(s):
        layer = 1 - lax.rem(s, 2)
        gather_wait(BWD, s, 0)
        back = dot_nt(gathered(BWD, s, 0), w_out[layer, :, pl.ds(0, HALF)])
        gather_wait(BWD, s, 1)
        back = back + dot_nt(gathered(BWD, s, 1), w_out[layer, :, pl.ds(HALF, HALF)])
        back_hidden = (back * slope_k[...]).astype(BF16)
        back_h[s] = back_hidden
        for h in range(2):
            put_part(BWD, h, dot_nt(back_hidden, w_in[layer, pl.ds(h * HALF, HALF)]))

    def forward_rows(s):
        tick, k = s // 2, lax.rem(s, 2)
        branch = whole_sum(FWD, k)
        for h in range(2):
            rows[tick, FWD, k + 2, h] = (rows[tick, FWD, k, h].astype(F32) - branch[h]).astype(BF16)

    def backward_rows(s):
        tick, k = s // 2, lax.rem(s, 2)
        scale, unit = norm_of(tick, k + 1)
        gain = gain_row(1 - k)
        back_normed = whole_sum(BWD, k)
        back_unit = [back_normed[h] * gain[:, h * HALF : (h + 1) * HALF] for h in range(2)]
        mean = (
            jnp.sum(back_unit[0] * unit[0], axis=-1, keepdims=True)
            + jnp.sum(back_unit[1] * unit[1], axis=-1, keepdims=True)
        ) * (1.0 / (2 * HALF))
        for h in range(2):
            back_input = scale * (back_unit[h] - unit[h] * mean)
            rows[tick, BWD, k + 2, h] = (rows[tick, BWD, k, h].astype(F32) + back_input).astype(BF16)

    def rows_and_next(s):
        forward_rows(s)
        for k in range(2):
            pl.when(s == k)(lambda k=k: hand_on(FWD, k))
        pl.when(lax.rem(s, 2) == 0)(lambda: begin(FWD, s + 1))
        pl.when(s == 3)(lambda: put_rows(1, 0))
        backward_rows(s)
        for k in range(2):
            pl.when(s == k)(lambda k=k: hand_on(BWD, k))
        pl.when(lax.rem(s, 2) == 0)(lambda: begin(BWD, s + 1))

        @pl.when(s == 1)
        def _():
            for chain in (FWD, BWD):
                take_over(chain)
                begin(chain, 2)

    def grad_out(layer):
        for h in range(2):
            first, second = 1 - layer, 3 - layer
            g_out = dot_nn(act_t[first], gathered(BWD, first, h)) + dot_nn(act_t[second], gathered(BWD, second, h))
            gw_out[layer, :, pl.ds(h * HALF, HALF)] = g_out.astype(BF16)

    def grad_in(layer):
        for h in range(2):
            first, second = 1 - layer, 3 - layer
            span = pl.ds(h * HALF, HALF)
            g_in = dot_tn(gathered(FWD, first, h), back_h[first]) + dot_tn(gathered(FWD, second, h), back_h[second])
            gw_in[layer, span] = g_in.astype(BF16)
            product = (g_in * w_in[layer, span].astype(F32)).astype(BF16)
            sums = dot_nt(jnp.ones((8, 256), BF16), product)
            gain_sum[2 * layer + h] = sums / gains[0, layer : layer + 1, h * HALF : (h + 1) * HALF]

    def out_copy(layer, which):
        if which == 0:
            return pltpu.make_async_copy(gw_in.at[layer], grad_in_hbm.at[layer], out_s.at[layer, 0])
        return pltpu.make_async_copy(gw_out.at[layer], grad_out_hbm.at[layer], out_s.at[layer, 1])

    def put_rows(tick, j):
        chain, place = ((FWD, 3), (FWD, 2), (BWD, 2), (BWD, 3))[j]
        for h in range(2):
            v = rows[tick, chain, place, h].astype(F32)
            rebuilt[tick, j, :, h * HALF : (h + 1) * HALF] = jnp.where(z == 0, v[:8], v[8:]).astype(BF16)

    def while_first_sum():
        for layer in (1, 0):
            grad_in(layer)
            out_copy(layer, 0).start()
        mine = [gain_sum[j, 0:1] for j in range(4)]
        grx[x] = jnp.concatenate(mine + mine, axis=0)
        for d in (1, 2, 3):
            send(grx.at[x], grx.at[x], gx_s.at[0], gx_r.at[0], x_peer(d))

    def while_second_sum():
        wait(grx.at[pl.ds(0, 3)], gx_r.at[0])
        gry[y] = (grx[0] + grx[1]) + (grx[2] + grx[3])
        for d in (1, 2, 3):
            send(gry.at[y], gry.at[y], gx_s.at[1], gx_r.at[1], y_peer(d))
        for layer in (1, 0):
            grad_out(layer)
            out_copy(layer, 1).start()

    def while_third_sum():
        wait(gry.at[pl.ds(0, 3)], gx_r.at[1])
        grz[0] = (gry[0] + gry[1]) + (gry[2] + gry[3])
        send(grz.at[0], grz.at[1], gx_s.at[2], gx_r.at[2], z_peer)
        for j in range(4):
            put_rows(0, j)
        put_rows(1, 1)
        put_rows(1, 2)

    def step(s, carry):
        k = lax.rem(s, 2)
        gather_mid(FWD, s)
        gather_mid(BWD, s)
        gather_pass(FWD, s)
        gather_pass(BWD, s)
        forward(s)
        backward(s)
        sum_pass(FWD)
        sum_pass(BWD)
        pl.when(s == 3)(while_first_sum)
        gather_sent(FWD, s)
        gather_sent(BWD, s)
        sum_mid(FWD)
        sum_mid(BWD)
        pl.when(s == 3)(while_second_sum)
        sum_end(FWD, k)
        sum_end(BWD, k)
        pl.when(s == 3)(while_third_sum)
        rows_and_next(s)
        sum_sent(FWD)
        sum_sent(BWD)
        return carry

    lax.fori_loop(0, 4, step, 0)

    put_rows(1, 3)
    wait(grz.at[1], gx_r.at[2])
    total = grz[0] + grz[1]
    for layer in range(2):
        for h in range(2):
            grad_gains[0, layer : layer + 1, h * HALF : (h + 1) * HALF] = total[2 * layer + h : 2 * layer + h + 1]

    wait(grx.at[pl.ds(0, 3)], gx_s.at[0])
    wait(gry.at[pl.ds(0, 3)], gx_s.at[1])
    wait(grz.at[0], gx_s.at[2])
    for j in range(4):
        wait(hs.at[0, j], hs_s.at[j])

    @pl.when(sec == last)
    def _():
        for j in range(4):
            wait(hs.at[1, j], hs_s.at[4 + j])

    @pl.when(sec > 0)
    def _():
        for chain in range(2):
            for k in range(2):
                wait(rows.at[0, chain, k + 2], tick_s.at[chain, k])

    for layer in range(2):
        for which in range(2):
            out_copy(layer, which).wait()


def write_out(*refs):
    sources, results, held, sems = refs[:4], refs[4:8], refs[8:12], refs[12]

    def pieces(first, second):
        found = [(0, ...), (3, ...)]
        for layer in range(2):
            for j in range(4):
                found.append((1, (layer, pl.ds(512 * j, 512))))
                found.append((2, (layer, pl.ds(64 * j, 64))))
        return [
            pltpu.make_async_copy(first[i].at[at], second[i].at[at], sems.at[n, 0 if second is held else 1])
            for n, (i, at) in enumerate(found)
        ]

    loads, stores = pieces(sources, held), pieces(held, results)
    for load in loads:
        load.start()
    for load, store in zip(loads, stores):
        load.wait()
        store.start()
    for store in stores:
        store.wait()


def per_device(held, head, gains, w_in, w_out, masks):
    vmem = pl.BlockSpec(memory_space=pltpu.VMEM)
    anywhere = pl.BlockSpec(memory_space=pl.ANY)
    dma = pltpu.SemaphoreType.DMA
    shapes = (
        jax.ShapeDtypeStruct((2, 4, 8, 2 * HALF), BF16),
        jax.ShapeDtypeStruct((2, 2 * HALF, 256), BF16),
        jax.ShapeDtypeStruct((2, 256, 2 * HALF), BF16),
        jax.ShapeDtypeStruct((1, 2, 2 * HALF), F32),
    )
    results = pl.pallas_call(
        kernel,
        out_shape=shapes,
        in_specs=[anywhere] * 6,
        out_specs=(vmem, anywhere, anywhere, vmem),
        scratch_shapes=[
            pltpu.VMEM((2, 2 * HALF, 256), BF16),
            pltpu.VMEM((2, 256, 2 * HALF), BF16),
            pltpu.VMEM((4, 8, 2 * HALF), BF16),
            pltpu.VMEM((4, 8, 2 * HALF), BF16),
            pltpu.VMEM((1, 2, 2 * HALF), F32),
            pltpu.VMEM((2, 2 * HALF, 256), BF16),
            pltpu.VMEM((2, 256, 2 * HALF), BF16),
            pltpu.VMEM((2, 2, 16, 2, 8, 256), jnp.int32),
            pltpu.VMEM((4, 2, 2, 4, 4, 16, HALF), BF16),
            pltpu.VMEM((2, 2, 4, 4, 16, HALF), BF16),
            pltpu.VMEM((2, 2, 2, 4, 16, HALF), BF16),
            pltpu.VMEM((2, 2, 4, 16, HALF), BF16),
            pltpu.VMEM((2, 2, 3, 16, HALF), BF16),
            pltpu.VMEM((2, 2, 16, HALF), BF16),
            pltpu.VMEM((2, 2, 2, 16, HALF), BF16),
            pltpu.VMEM((2, 2, 2, 4, 16, QUARTER), BF16),
            pltpu.VMEM((2, 2, 4, 2, 16, HALF), BF16),
            pltpu.VMEM((4, 256, 256), BF16),
            pltpu.VMEM((4, 256, 256), BF16),
            pltpu.VMEM((256, 256), F32),
            pltpu.VMEM((2, 4, 16, HALF), BF16),
            pltpu.VMEM((2, 4, 16, HALF), BF16),
            pltpu.VMEM((4, 8, HALF), F32),
            pltpu.VMEM((4, 8, HALF), F32),
            pltpu.VMEM((4, 8, HALF), F32),
            pltpu.VMEM((2, 8, HALF), F32),
            dma((2, 2)), dma((2, 2)),
            dma((2, 2)), dma((2, 2)),
            dma((2, 2)), dma((2, 2, 2)), dma((2, 2)), dma((2, 2)), dma((2, 2)),
            dma((2, 2)), dma((2, 2)), dma((2, 2, 2)), dma((2, 2)), dma((2, 2)),
            dma((2, 2)), dma((2, 2)),
            dma((2,)), dma((2, 2)),
            dma((2, 2)), dma((2, 2)),
            dma((8,)), dma((8,)),
            dma((3,)), dma((3,)),
            dma((21,)),
            dma((2, 2)),
        ],
        compiler_params=pltpu.CompilerParams(
            collective_id=0, has_side_effects=True, vmem_limit_bytes=VMEM_BYTES
        ),
        name="relay",
    )(held[0], head, gains, w_in[0], w_out[0], masks.reshape(2, 2, 2, 16, 8, 256))
    rebuilt, grad_in, grad_out, grad_gains = pl.pallas_call(
        write_out,
        out_shape=shapes,
        in_specs=[anywhere] * 4,
        out_specs=(anywhere,) * 4,
        scratch_shapes=[pltpu.VMEM(shape.shape, shape.dtype) for shape in shapes] + [dma((18, 2))],
        compiler_params=pltpu.CompilerParams(vmem_limit_bytes=VMEM_BYTES),
        name="write_out",
    )(*results)
    return rebuilt[None], grad_in[None], grad_out[None], grad_gains


def solution(mesh):
    return jax.shard_map(
        per_device,
        mesh=mesh,
        in_specs=(
            P("section", None, "tensor", None),
            P(None, "tensor", None),
            P("section", None, None),
            P("section", None, None, "tensor"),
            P("section", None, "tensor", None),
            P("section", None, None, None, "tensor"),
        ),
        out_specs=(
            P("section", None, None, "tensor", None),
            P("section", None, None, "tensor"),
            P("section", None, "tensor", None),
            P("section", None, None),
        ),
        check_vma=False,
    )
```
